32 devices in a mesh: groups: 2 (over y), tensor: 4 (over x, core), dp: 4 (over z).
Axes of the slice: x: 2, y: 2, z: 4, core: 2. Of those that a mesh axis runs over, the one named last changes fastest.
Arguments:
- hidden_input: bfloat16 [2048, 8192], P(('groups', 'dp'), 'tensor'), parts along dimension 0, may hold values from -6 to 6
- input_weight: bfloat16 [8192, 8192], P(None, 'tensor'), may hold values from -0.0625 to 0.0625
- kernel_weight: float32 [4, 8192], P(None, 'tensor'), may hold values from -3 to 3
- kernel_bias: float32 [8192], P('tensor'), may hold values from -3 to 3
- select_weight: bfloat16 [8192, 544], P('tensor'), may hold values from -0.0625 to 0.0625
- step_gain: float32 [512], replicated, may hold values from 0.1 to 1.9
- step_weight: bfloat16 [512, 8192], P(None, 'tensor'), may hold values from -0.25 to 0.25
- step_bias: float32 [8192], P('tensor'), may hold values from -6 to -2
- decay_log: float32 [16, 8192], P(None, 'tensor'), may hold values from 0 to 2.77
- skip_gain: float32 [8192], P('tensor'), may hold values from 0.5 to 1.5
- state_cache: bfloat16 [640, 16, 8192], P(('groups', 'dp'), None, 'tensor'), parts along dimension 0, may hold values from -3 to 3
- window_cache: bfloat16 [640, 3, 8192], P(('groups', 'dp'), None, 'tensor'), parts along dimension 0, may hold values from -6 to 6
- cache_owner: int32 [512], P(('groups', 'dp')), parts along dimension 0, may hold values from 0 to 3, as said below
- cache_slot: int32 [512], P(('groups', 'dp')), parts along dimension 0, may hold values from 0 to 79, as said below
- accepted: int32 [512], P(('groups', 'dp')), parts along dimension 0, may hold values from 0 to 4
Outputs:
- mamba_output: bfloat16 [2048, 8192], P(('groups', 'dp'), 'tensor'), parts along dimension 0
- new_state_cache: bfloat16 [640, 16, 8192], P(('groups', 'dp'), None, 'tensor'), parts along dimension 0
- new_window_cache: bfloat16 [640, 3, 8192], P(('groups', 'dp'), None, 'tensor'), parts along dimension 0
The draws below stay inside these ranges and needn't reach their ends.
There are 2 independent parts, one for each index of `groups`. The reference program is written for one: setup_inputs(seed, part) draws one part's arguments, and reference() takes and returns one part's arrays. A program takes and returns all parts, laid end to end along the dimension named above; an argument that names none is the same for every part. Nothing has to cross between parts.
Inputs may be any that keep to these rules, and one draw needn't show every extreme that they name: `cache_owner`: at most 32 requests of one index of dp share an owner, and among the requests of every index of dp some owner has exactly 32; every owner holds exactly 64 requests. `cache_slot`: no two requests share both owner and slot.
All inputs are finite; a program needn't handle non-finite values.
Results may differ from the reference program's by a relative error of at most 0.0095.
Values may be sent and summed in bfloat16 or wider, within the bound.
A program may use at most 192 MiB of HBM per device.

```python
import jax
import jax.numpy as jnp
from jax import lax

D = 8192
E = 8192
R = 512
N = 16
KER = 4
DRAFT = 4
REQ_DEV = 64
SLOTS_DEV = 80
REQS = 256
SLOTS = 320
TOKENS = 1024
PROJ = 544
N_DP = 4


def route_table(key):
    owners_total = N_DP
    capacity = 2 * REQ_DEV // N_DP
    remaining = REQ_DEV - capacity
    split_keys = jax.random.split(key, 5)
    weights = jax.random.randint(split_keys[0], (owners_total - 1,), 1, 3)
    edges = remaining * jnp.concatenate([jnp.zeros((1,), jnp.int32), jnp.cumsum(weights)]) // jnp.sum(weights)
    base_counts = jnp.concatenate([jnp.full((1,), capacity, jnp.int32), edges[1:] - edges[:-1]])
    row_order = jax.random.permutation(split_keys[1], owners_total)
    column_order = jax.random.permutation(split_keys[2], owners_total)
    counts = base_counts[(row_order[:, None] + column_order[None, :]) % owners_total]
    bounds = jnp.cumsum(counts, axis=1)
    sorted_owner = jnp.sum((jnp.arange(REQ_DEV)[None, :, None] >= bounds[:, None, :]).astype(jnp.int32), axis=2)
    shuffles = jax.vmap(lambda subkey: jax.random.permutation(subkey, REQ_DEV))(jax.random.split(split_keys[3], owners_total))
    owners = jnp.take_along_axis(sorted_owner, shuffles, axis=1)
    matches = (owners[:, :, None] == jnp.arange(owners_total)[None, None, :]).astype(jnp.int32)
    within = jnp.sum((jnp.cumsum(matches, axis=1) - matches) * matches, axis=2)
    earlier = jnp.cumsum(counts, axis=0) - counts
    position = within + jnp.take_along_axis(earlier, owners, axis=1)
    slot_orders = jax.vmap(lambda subkey: jax.random.permutation(subkey, SLOTS_DEV))(jax.random.split(split_keys[4], owners_total))
    slots = slot_orders[owners, position]
    return (owners.reshape(-1).astype(jnp.int32), slots.reshape(-1).astype(jnp.int32))


def draw_cache_owner(key, part):
    table = route_table(key)
    return table[0]


def draw_cache_slot(key, part):
    table = route_table(key)
    return table[1]


def place_ends(array, stream_key, least, largest):
    spot = [jax.random.randint(jax.random.fold_in(stream_key, axis), (), 0, length) for axis, length in enumerate(array.shape)]
    main_axis = array.shape.index(max(array.shape))
    next_to = spot[:main_axis] + [(spot[main_axis] + 1) % array.shape[main_axis]] + spot[main_axis + 1:]
    return array.at[tuple(spot)].set(least).at[tuple(next_to)].set(largest)


def block_levels(rng, shape, cuts, smallest, largest):
    def one(axis_at, parts):
        draws = jax.random.uniform(jax.random.fold_in(jax.random.fold_in(rng, 6), axis_at), (parts,), jnp.float32, smallest / len(cuts), largest / len(cuts))
        return jnp.repeat(jnp.exp(draws), shape[axis_at] // parts).reshape((-1,) + (1,) * (len(shape) - axis_at - 1))

    loudness = one(*cuts[0])
    for cut in cuts[1:]:
        loudness = loudness * one(*cut)
    return loudness


def normal_values(own_key, shape, spread, bound, cuts=(), held_as=jnp.bfloat16):
    drawn = spread * jax.random.normal(own_key, shape, jnp.float32)
    if cuts:
        drawn = drawn * block_levels(own_key, shape, cuts, -0.22, 0.18)
    return jnp.clip(drawn, -bound, bound).astype(held_as)


def setup_inputs(seed: int = 0, part: int = 0) -> dict:
    splits = jax.random.split(jax.random.key(seed), 16)
    part_keys = jax.random.split(jax.random.fold_in(splits[15], part), 16)
    return {
        "hidden_input": normal_values(part_keys[0], (TOKENS, D), 1.0, 6.0, ((0, 4), (1, 4))),
        "input_weight": normal_values(splits[1], (D, E), D ** -0.5, 0.0625, ((1, 4),)),
        "kernel_weight": normal_values(splits[2], (KER, E), KER ** -0.5, 3.0, ((1, 4),), jnp.float32),
        "kernel_bias": normal_values(splits[3], (E,), 0.5, 3.0, ((0, 4),), jnp.float32),
        "select_weight": normal_values(splits[4], (E, PROJ), E ** -0.5, 0.0625, ((0, 4),)),
        "step_gain": jnp.clip(1.0 + 0.18 * jax.random.normal(splits[5], (R,), jnp.float32), 0.1, 1.9),
        "step_weight": normal_values(splits[6], (R, E), R ** -0.5, 0.25, ((1, 4),)),
        "step_bias": jnp.clip(-6.0 + 4.0 * jax.random.uniform(splits[7], (E,), jnp.float32) ** block_levels(splits[7], (E,), ((0, 4),), -0.2, 0.2), -6.0, -2.0),
        "decay_log": jnp.clip(2.77 * jax.random.uniform(splits[8], (N, E), jnp.float32) ** block_levels(splits[8], (N, E), ((1, 4),), -0.2, 0.2), 0.0, 2.77),
        "skip_gain": jnp.clip(0.5 + 1.0 * jax.random.uniform(splits[9], (E,), jnp.float32) ** block_levels(splits[9], (E,), ((0, 4),), -0.2, 0.2), 0.5, 1.5),
        "state_cache": normal_values(part_keys[10], (SLOTS, N, E), 0.5, 3.0, ((0, 4), (2, 4))),
        "window_cache": normal_values(part_keys[11], (SLOTS, KER - 1, E), 1.0, 6.0, ((0, 4), (2, 4))),
        "cache_owner": draw_cache_owner(jax.random.fold_in(jax.random.fold_in(splits[15], part), 71), part),
        "cache_slot": draw_cache_slot(jax.random.fold_in(jax.random.fold_in(splits[15], part), 71), part),
        "accepted": place_ends(jax.random.randint(part_keys[14], (REQS,), 0, 5), jax.random.fold_in(part_keys[14], 1), 0, 4).astype(jnp.int32),
    }


epsilon = 1e-06

def recur(carried, activated, step_size, state_input, state_output, decay_log, skip_gain, accepted):
    decay = -jnp.exp(decay_log)
    accepted_state = carried
    token_outputs = []
    for position in range(activated.shape[1]):
        step_now = step_size[:, position]
        input_now = activated[:, position].astype(jnp.float32)
        carried = jnp.exp(step_now[:, None, :] * decay[None]) * carried + (step_now * input_now)[:, None, :] * state_input[:, position, :, None]
        token_outputs.append(jnp.einsum('mn,mne->me', state_output[:, position], carried) + skip_gain * input_now)
        accepted_state = jnp.where((accepted == position + 1)[:, None, None], carried, accepted_state)
    return (jnp.stack(token_outputs, axis=1).astype(jnp.bfloat16), accepted_state.astype(jnp.bfloat16))

def roll_window(window, accepted, kept_taps):
    selected = window[:, 0:kept_taps]
    for position in range(1, window.shape[1] - kept_taps + 1):
        selected = jnp.where((accepted == position)[:, None, None], window[:, position:position + kept_taps], selected)
    return selected

def reference(hidden_input, input_weight, kernel_weight, kernel_bias, select_weight, step_gain, step_weight, step_bias, decay_log, skip_gain, state_cache, window_cache, cache_owner, cache_slot, accepted):
    inputs = jnp.dot(hidden_input, input_weight, preferred_element_type=jnp.float32).astype(jnp.bfloat16).reshape(REQS, DRAFT, E)
    cache_rows = (cache_owner * SLOTS_DEV + cache_slot).astype(jnp.int32)
    carried = state_cache[cache_rows].astype(jnp.float32)
    window = jnp.concatenate([window_cache[cache_rows], inputs], axis=1)
    mixed = kernel_bias + kernel_weight[0] * window[:, 0:DRAFT].astype(jnp.float32)
    for tap_index in range(1, KER):
        mixed = mixed + kernel_weight[tap_index] * window[:, tap_index:tap_index + DRAFT].astype(jnp.float32)
    activated = jax.nn.silu(mixed).astype(jnp.bfloat16)
    projected = jnp.dot(activated.reshape(REQS * DRAFT, E), select_weight, preferred_element_type=jnp.float32)
    rank_part = projected[:, :R]
    norm_scale = lax.rsqrt(lax.optimization_barrier(jnp.mean(rank_part * rank_part, axis=1, keepdims=True)) + epsilon)
    rank_normed = (rank_part * norm_scale * step_gain).astype(jnp.bfloat16)
    step_size = jax.nn.softplus(jnp.dot(rank_normed, step_weight, preferred_element_type=jnp.float32) + step_bias).reshape(REQS, DRAFT, E)
    state_input = projected[:, R:R + N].reshape(REQS, DRAFT, N)
    state_output = projected[:, R + N:].reshape(REQS, DRAFT, N)
    mamba_output, accepted_state = recur(carried, activated, step_size, state_input, state_output, decay_log, skip_gain, accepted)
    rolled = roll_window(window, accepted, KER - 1)
    new_state_cache = state_cache.at[cache_rows].set(accepted_state)
    new_window_cache = window_cache.at[cache_rows].set(rolled)
    return (mamba_output.reshape(REQS * DRAFT, E), new_state_cache, new_window_cache)
```

```python
import jax
import jax.numpy as jnp
from jax import lax
from jax.sharding import PartitionSpec as P

epsilon = 1e-06


def one_hot_rows(row_code, column_code):
    return (row_code[:, None] == column_code[None, :]).astype(jnp.bfloat16)


def move_rows(selector, rows):
    return jnp.dot(selector, rows, preferred_element_type=jnp.float32).astype(jnp.bfloat16)


def routing(cache_owner, cache_slot, accepted, slots_here):
    owner_count = lax.axis_size("dp")
    here = lax.axis_index("dp")
    request_count = cache_owner.shape[0]
    capacity = 2 * request_count // owner_count
    place = cache_owner * slots_here + cache_slot
    everyone = lax.all_gather(place * 8 + accepted, "dp", axis=0, tiled=False)
    earlier = jnp.tril(jnp.ones((request_count, request_count), jnp.int32), -1)
    place_all = everyone // 8
    owner_all = place_all // slots_here
    same = (owner_all[:, :, None] == owner_all[:, None, :]).astype(jnp.int32)
    within_all = jnp.sum(same * earlier[None], axis=2)
    mine = (owner_all == here).reshape(-1)
    slot_all = jnp.where(mine, (place_all - here * slots_here).reshape(-1), -1)
    packed_all = (jnp.arange(owner_count)[:, None] * capacity + within_all).reshape(-1)
    match = slot_all[None, :] == jnp.arange(slots_here)[:, None]
    slot_source = jnp.max(jnp.where(match, packed_all[None, :], -1), axis=1)
    slot_accepted = jnp.max(jnp.where(match, (everyone % 8).reshape(-1)[None, :], 0), axis=1)
    own_same = (cache_owner[:, None] == cache_owner[None, :]).astype(jnp.int32)
    send_row = cache_owner * capacity + jnp.sum(own_same * earlier, axis=1)
    return send_row, slot_source, slot_accepted, capacity


def on_device(
    hidden_input,
    input_weight,
    kernel_weight,
    kernel_bias,
    select_weight,
    step_gain,
    step_weight,
    step_bias,
    decay_log,
    skip_gain,
    state_cache,
    window_cache,
    cache_owner,
    cache_slot,
    accepted,
):
    owner_count = lax.axis_size("dp")
    slots, states, channels = state_cache.shape
    kept = window_cache.shape[1]
    request_count = cache_owner.shape[0]
    tokens = hidden_input.shape[0] // request_count
    send_row, slot_source, slot_accepted, capacity = routing(
        cache_owner, cache_slot, accepted, slots
    )
    packed = owner_count * capacity
    token_axis = jnp.arange(tokens, dtype=jnp.int32)
    request_code = (send_row[:, None] * tokens + token_axis[None, :]).reshape(-1)
    packed_index = jnp.arange(packed, dtype=jnp.int32).reshape(owner_count, 1, capacity)
    packed_code = (packed_index * tokens + token_axis[None, :, None]).reshape(-1)
    slot_code = jnp.where(
        slot_source[None, :] >= 0, slot_source[None, :] * tokens + token_axis[:, None], -1
    ).reshape(-1)

    outgoing = move_rows(one_hot_rows(packed_code, request_code), hidden_input)
    outgoing = outgoing.reshape(owner_count, tokens * capacity, -1)
    arrived = lax.all_to_all(outgoing, "dp", split_axis=0, concat_axis=0, tiled=True)
    placed = move_rows(
        one_hot_rows(slot_code, packed_code), arrived.reshape(packed * tokens, -1)
    )
    gathered = lax.all_gather(placed, "tensor", axis=1, tiled=True)
    inputs = jnp.dot(gathered, input_weight, preferred_element_type=jnp.float32).astype(
        jnp.bfloat16
    ).reshape(tokens, slots, channels)
    old_window = jnp.transpose(window_cache, (1, 0, 2))
    window = jnp.concatenate([old_window, inputs], axis=0)
    mixed = kernel_bias + kernel_weight[0] * window[0:tokens].astype(jnp.float32)
    for tap in range(1, kernel_weight.shape[0]):
        mixed = mixed + kernel_weight[tap] * window[tap : tap + tokens].astype(jnp.float32)
    activated = jax.nn.silu(mixed).astype(jnp.bfloat16)
    rolled = window[0:kept]
    for position in range(1, tokens + 1):
        rolled = jnp.where(
            (slot_accepted == position)[None, :, None], window[position : position + kept], rolled
        )
    new_window_cache = jnp.transpose(rolled, (1, 0, 2))

    partial_value = jnp.dot(
        activated.reshape(tokens * slots, channels),
        select_weight,
        preferred_element_type=jnp.float32,
    )
    projected = lax.psum(partial_value, "tensor")
    rank = step_gain.shape[0]
    rank_part = projected[:, :rank]
    norm_scale = lax.rsqrt(jnp.mean(rank_part * rank_part, axis=1, keepdims=True) + epsilon)
    rank_normed = (rank_part * norm_scale * step_gain).astype(jnp.bfloat16)
    step_size = jax.nn.softplus(
        jnp.dot(rank_normed, step_weight, preferred_element_type=jnp.float32) + step_bias
    ).reshape(tokens, slots, channels)
    state_input = projected[:, rank : rank + states].reshape(tokens, slots, states)
    state_output = projected[:, rank + states :].reshape(tokens, slots, states)

    decay = -jnp.exp(decay_log)
    carried = state_cache.astype(jnp.float32)
    kept_state = carried
    outputs = []
    for t in range(tokens):
        step_now = step_size[t]
        input_now = activated[t].astype(jnp.float32)
        carried = (
            jnp.exp(step_now[:, None, :] * decay[None]) * carried
            + (step_now * input_now)[:, None, :] * state_input[t][:, :, None]
        )
        outputs.append(
            jnp.sum(state_output[t][:, :, None] * carried, axis=1) + skip_gain * input_now
        )
        kept_state = jnp.where((slot_accepted == t + 1)[:, None, None], carried, kept_state)
    new_state_cache = kept_state.astype(jnp.bfloat16)
    outputs = jnp.stack(outputs, axis=0).astype(jnp.bfloat16).reshape(tokens * slots, channels)

    returning = move_rows(one_hot_rows(packed_code, slot_code), outputs)
    returning = returning.reshape(owner_count, tokens * capacity, channels)
    returned = lax.all_to_all(returning, "dp", split_axis=0, concat_axis=0, tiled=True)
    mamba_output = move_rows(
        one_hot_rows(request_code, packed_code), returned.reshape(packed * tokens, channels)
    )
    return mamba_output, new_state_cache, new_window_cache


def solution(mesh):
    in_specs = (
        P(("groups", "dp"), "tensor"),
        P(None, "tensor"),
        P(None, "tensor"),
        P("tensor"),
        P("tensor", None),
        P(),
        P(None, "tensor"),
        P("tensor"),
        P(None, "tensor"),
        P("tensor"),
        P(("groups", "dp"), None, "tensor"),
        P(("groups", "dp"), None, "tensor"),
        P(("groups", "dp")),
        P(("groups", "dp")),
        P(("groups", "dp")),
    )
    out_specs = (
        P(("groups", "dp"), "tensor"),
        P(("groups", "dp"), None, "tensor"),
        P(("groups", "dp"), None, "tensor"),
    )
    return jax.shard_map(
        on_device, mesh=mesh, in_specs=in_specs, out_specs=out_specs, check_vma=False
    )
```

```python
import functools
import math

import jax
import jax.numpy as jnp
from jax import lax
from jax.experimental import pallas as pl
from jax.experimental.pallas import tpu as pltpu
from jax.sharding import PartitionSpec as P

epsilon = 1e-06


def routing(cache_owner, cache_slot, accepted, slots_here):
    owner_count = lax.axis_size("dp")
    here = lax.axis_index("dp")
    request_count = cache_owner.shape[0]
    capacity = 2 * request_count // owner_count
    place = cache_owner * slots_here + cache_slot
    everyone = lax.all_gather(place * 8 + accepted, "dp", axis=0, tiled=False)
    earlier = jnp.tril(jnp.ones((request_count, request_count), jnp.int32), -1)
    place_all = everyone // 8
    owner_all = place_all // slots_here
    same = (owner_all[:, :, None] == owner_all[:, None, :]).astype(jnp.int32)
    within_all = jnp.sum(same * earlier[None], axis=2)
    mine = (owner_all == here).reshape(-1)
    slot_all = jnp.where(mine, (place_all - here * slots_here).reshape(-1), -1)
    packed_all = (jnp.arange(owner_count)[:, None] * capacity + within_all).reshape(-1)
    match = slot_all[None, :] == jnp.arange(slots_here)[:, None]
    slot_source = jnp.max(jnp.where(match, packed_all[None, :], -1), axis=1)
    slot_accepted = jnp.max(jnp.where(match, (everyone % 8).reshape(-1)[None, :], 0), axis=1)
    own_same = (cache_owner[:, None] == cache_owner[None, :]).astype(jnp.int32)
    send_row = cache_owner * capacity + jnp.sum(own_same * earlier, axis=1)
    return send_row, slot_source, slot_accepted, capacity


MESH = pl.DeviceIdType.MESH
VMEM_LIMIT = 60 * 1024 * 1024


def match(left, right):
    return (left == right).astype(jnp.bfloat16)


def product(left, right):
    return jnp.dot(left, right, preferred_element_type=jnp.float32)


def project_kernel(
    sizes,
    hidden_ref,
    weight_ref,
    request_ref,
    slot_ref,
    base_col_ref,
    base_row_ref,
    out_ref,
    send,
    recv,
    gath,
    wbuf,
    acc,
    w_sem,
    z_send,
    z_recv,
    x_send,
    x_recv,
    s_send,
    s_recv,
):
    owners, lines, chunks, width, block, columns = sizes
    dp = lax.axis_index("dp")
    tensor = lax.axis_index("tensor")
    line = tensor // 2
    core = tensor % 2
    depth = width * chunks

    def origin(step):
        return ((line + lines - step // 2) % lines) * 2 + (core + step) % 2

    weights = []
    for k in range(chunks):
        for g in range(2 * lines):
            first = pl.multiple_of(origin(g) * depth + k * width, width)
            copy = pltpu.make_async_copy(
                weight_ref.at[pl.ds(first, width)], wbuf.at[k, g], w_sem.at[k, g]
            )
            copy.start()
            weights.append(copy)

    barrier = pltpu.get_barrier_semaphore()
    sibling = line * 2 + 1 - core
    pl.semaphore_signal(barrier, inc=1, device_id={"tensor": sibling}, device_id_type=MESH)
    for j in range(1, owners):
        pl.semaphore_signal(
            barrier, inc=1, device_id={"dp": (dp + j) % owners}, device_id_type=MESH
        )
    for j in range(1, lines):
        pl.semaphore_signal(
            barrier,
            inc=1,
            device_id={"tensor": ((line + j) % lines) * 2 + core},
            device_id_type=MESH,
        )
    pl.semaphore_wait(barrier, owners + lines - 1)

    across = {}
    for k in range(chunks):
        part = pl.ds(k * width, width)
        for j in list(range(1, owners)) + [0]:
            target = (dp + j) % owners
            pick = match(base_col_ref[...] + target * block, request_ref[...])
            rows = product(pick, hidden_ref[:, part]).astype(jnp.bfloat16)
            if j == 0:
                recv[k, 0] = rows
            else:
                send[k, j] = rows
                copy = pltpu.make_async_remote_copy(
                    src_ref=send.at[k, j],
                    dst_ref=recv.at[k, j],
                    send_sem=z_send.at[k, j],
                    recv_sem=z_recv.at[k, j],
                    device_id={"dp": target},
                    device_id_type=MESH,
                )
                copy.start()
                across[k, j] = copy

    strip = min(512, columns)

    def multiply(k, g):
        weights[k * 2 * lines + g].wait()

        def body(c, _):
            at = pl.ds(pl.multiple_of(c * strip, strip), strip)
            value = product(gath[k, g], wbuf[k, g, :, at])
            if k == 0 and g == 0:
                acc[:, at] = value
            else:
                acc[:, at] += value
            return 0

        lax.fori_loop(0, columns // strip, body, 0)

    sideways, shared = {}, {}

    def share(k, g):
        copy = pltpu.make_async_remote_copy(
            src_ref=gath.at[k, g],
            dst_ref=gath.at[k, g + 1],
            send_sem=s_send.at[k, g],
            recv_sem=s_recv.at[k, g],
            device_id={"tensor": sibling},
            device_id_type=MESH,
        )
        copy.start()
        shared[k, g] = copy

    def first(k):
        total = None
        for j in range(owners):
            if j:
                across[k, j].wait_recv()
            source = (dp + owners - j) % owners
            pick = match(slot_ref[...], base_row_ref[...] + source * block)
            value = product(pick, recv[k, j])
            total = value if total is None else total + value
        gath[k, 0] = total.astype(jnp.bfloat16)
        for j in range(1, lines):
            copy = pltpu.make_async_remote_copy(
                src_ref=gath.at[k, 0],
                dst_ref=gath.at[k, 2 * j],
                send_sem=x_send.at[k, j],
                recv_sem=x_recv.at[k, j],
                device_id={"tensor": ((line + j) % lines) * 2 + core},
                device_id_type=MESH,
            )
            copy.start()
            sideways[k, j] = copy
        share(k, 0)
        multiply(k, 0)

    def second(k):
        for j in range(1, lines):
            sideways[k, j].wait_recv()
            share(k, 2 * j)
        shared[k, 0].wait_recv()
        multiply(k, 1)
        for j in range(1, lines):
            multiply(k, 2 * j)

    def third(k):
        for j in range(1, lines):
            shared[k, 2 * j].wait_recv()
            multiply(k, 2 * j + 1)

    for step in range(chunks + 2):
        if step < chunks:
            first(step)
        if 1 <= step <= chunks:
            second(step - 1)
        if step >= 2:
            third(step - 2)
    out_ref[...] = acc[...].astype(jnp.bfloat16)
    for copy in list(across.values()) + list(sideways.values()) + list(shared.values()):
        copy.wait_send()


def project(hidden, weight, request_code, slot_code, base, owners, lines, block):
    rows, depth = hidden.shape
    columns = weight.shape[1]
    placed = slot_code.shape[0]
    chunks = 4
    width = depth // chunks
    groups = 2 * lines
    sizes = (owners, lines, chunks, width, block, columns)
    vmem = pl.BlockSpec(memory_space=pltpu.VMEM)
    dma = pltpu.SemaphoreType.DMA
    return pl.pallas_call(
        functools.partial(project_kernel, sizes),
        out_shape=jax.ShapeDtypeStruct((placed, columns), jnp.bfloat16),
        in_specs=[vmem, pl.BlockSpec(memory_space=pl.ANY)] + [vmem] * 4,
        out_specs=vmem,
        scratch_shapes=[
            pltpu.VMEM((chunks, owners, block, width), jnp.bfloat16),
            pltpu.VMEM((chunks, owners, block, width), jnp.bfloat16),
            pltpu.VMEM((chunks, groups, placed, width), jnp.bfloat16),
            pltpu.VMEM((chunks, groups, width, columns), jnp.bfloat16),
            pltpu.VMEM((placed, columns), jnp.float32),
            dma((chunks, groups)),
            dma((chunks, owners)),
            dma((chunks, owners)),
            dma((chunks, lines)),
            dma((chunks, lines)),
            dma((chunks, groups)),
            dma((chunks, groups)),
        ],
        compiler_params=pltpu.CompilerParams(
            collective_id=0, has_side_effects=True, vmem_limit_bytes=VMEM_LIMIT
        ),
        cost_estimate=pl.CostEstimate(
            flops=2 * placed * depth * groups * columns,
            bytes_accessed=2 * depth * groups * columns,
            transcendentals=0,
        ),
    )(hidden, weight, request_code[None, :], slot_code[:, None], base[:, None], base[None, :])


def return_kernel(
    sizes,
    rows_ref,
    request_ref,
    slot_ref,
    base_col_ref,
    base_row_ref,
    out_ref,
    send,
    recv,
    z_send,
    z_recv,
):
    owners, chunks, width, block = sizes
    dp = lax.axis_index("dp")
    barrier = pltpu.get_barrier_semaphore()
    for j in range(1, owners):
        pl.semaphore_signal(
            barrier, inc=1, device_id={"dp": (dp + j) % owners}, device_id_type=MESH
        )
    pl.semaphore_wait(barrier, owners - 1)
    across = {}
    for k in range(chunks):
        part = pl.ds(k * width, width)
        for j in list(range(1, owners)) + [0]:
            target = (dp + j) % owners
            pick = match(base_col_ref[...] + target * block, slot_ref[...])
            rows = product(pick, rows_ref[:, part]).astype(jnp.bfloat16)
            if j == 0:
                recv[k, 0] = rows
            else:
                send[k, j] = rows
                copy = pltpu.make_async_remote_copy(
                    src_ref=send.at[k, j],
                    dst_ref=recv.at[k, j],
                    send_sem=z_send.at[k, j],
                    recv_sem=z_recv.at[k, j],
                    device_id={"dp": target},
                    device_id_type=MESH,
                )
                copy.start()
                across[k, j] = copy
    for k in range(chunks):
        total = None
        for j in range(owners):
            if j:
                across[k, j].wait_recv()
            source = (dp + owners - j) % owners
            pick = match(request_ref[...], base_row_ref[...] + source * block)
            value = product(pick, recv[k, j])
            total = value if total is None else total + value
        out_ref[:, pl.ds(k * width, width)] = total.astype(jnp.bfloat16)
    for copy in across.values():
        copy.wait_send()


def send_back(rows, request_code, slot_code, base, owners, block):
    columns = rows.shape[1]
    chunks = 4
    width = columns // chunks
    vmem = pl.BlockSpec(memory_space=pltpu.VMEM)
    dma = pltpu.SemaphoreType.DMA
    return pl.pallas_call(
        functools.partial(return_kernel, (owners, chunks, width, block)),
        out_shape=jax.ShapeDtypeStruct((request_code.shape[0], columns), jnp.bfloat16),
        in_specs=[vmem] * 5,
        out_specs=vmem,
        scratch_shapes=[
            pltpu.VMEM((chunks, owners, block, width), jnp.bfloat16),
            pltpu.VMEM((chunks, owners, block, width), jnp.bfloat16),
            dma((chunks, owners)),
            dma((chunks, owners)),
        ],
        compiler_params=pltpu.CompilerParams(
            collective_id=1, has_side_effects=True, vmem_limit_bytes=VMEM_LIMIT
        ),
    )(rows, request_code[:, None], slot_code[None, :], base[:, None], base[None, :])


def mix_kernel(
    tokens,
    inputs_ref,
    window_ref,
    taps_ref,
    bias_ref,
    select_ref,
    accepted_ref,
    activated_ref,
    partial_ref,
    rolled_ref,
):
    kept, slots, width = window_ref.shape

    def row(position):
        if position < kept:
            return window_ref[position]
        return inputs_ref[pl.ds((position - kept) * slots, slots), :]

    window = [row(position) for position in range(kept + tokens)]
    wide = [value.astype(jnp.float32) for value in window]
    for t in range(tokens):
        mixed = bias_ref[...] + taps_ref[pl.ds(0, 1), :] * wide[t]
        for tap in range(1, taps_ref.shape[0]):
            mixed = mixed + taps_ref[pl.ds(tap, 1), :] * wide[t + tap]
        activated_ref[pl.ds(t * slots, slots), :] = (mixed * jax.nn.sigmoid(mixed)).astype(
            jnp.bfloat16
        )
    accepted = jnp.broadcast_to(accepted_ref[...], (slots, width))
    for place in range(kept):
        chosen = wide[place]
        for position in range(1, tokens + 1):
            chosen = jnp.where(accepted == position, wide[position + place], chosen)
        rolled_ref[place] = chosen.astype(jnp.bfloat16)
    value = lax.dot_general(
        activated_ref[...],
        select_ref[...],
        (((1,), (1,)), ((), ())),
        preferred_element_type=jnp.float32,
    )

    @pl.when(pl.program_id(0) == 0)
    def _():
        partial_ref[...] = value

    @pl.when(pl.program_id(0) > 0)
    def _():
        partial_ref[...] += value


def mix(inputs, window, kernel_weight, kernel_bias, select_rows, slot_accepted, tokens):
    kept, slots, channels = window.shape
    width = min(512, channels)
    return pl.pallas_call(
        functools.partial(mix_kernel, tokens),
        grid=(channels // width,),
        out_shape=(
            jax.ShapeDtypeStruct(inputs.shape, jnp.bfloat16),
            jax.ShapeDtypeStruct((inputs.shape[0], select_rows.shape[0]), jnp.float32),
            jax.ShapeDtypeStruct(window.shape, jnp.bfloat16),
        ),
        in_specs=[
            pl.BlockSpec((inputs.shape[0], width), lambda i: (0, i)),
            pl.BlockSpec((kept, slots, width), lambda i: (0, 0, i)),
            pl.BlockSpec((kernel_weight.shape[0], width), lambda i: (0, i)),
            pl.BlockSpec((1, width), lambda i: (0, i)),
            pl.BlockSpec((select_rows.shape[0], width), lambda i: (0, i)),
            pl.BlockSpec((slots, 1), lambda i: (0, 0)),
        ],
        out_specs=(
            pl.BlockSpec((inputs.shape[0], width), lambda i: (0, i)),
            pl.BlockSpec((inputs.shape[0], select_rows.shape[0]), lambda i: (0, 0)),
            pl.BlockSpec((kept, slots, width), lambda i: (0, 0, i)),
        ),
        compiler_params=pltpu.CompilerParams(vmem_limit_bytes=VMEM_LIMIT),
    )(inputs, window, kernel_weight, kernel_bias[None, :], select_rows, slot_accepted[:, None])


def recur_kernel(
    tokens,
    accepted_ref,
    projected_ref,
    gain_ref,
    step_weight_ref,
    step_bias_ref,
    decay_ref,
    skip_ref,
    activated_ref,
    state_ref,
    into_ref,
    outof_ref,
    out_ref,
    new_state_ref,
    normed,
    step,
    scaled,
    result,
    rate,
):
    slots, states, width = state_ref.shape

    @pl.when(pl.program_id(0) == 0)
    def _():
        rank = gain_ref.shape[1]
        part = projected_ref[:, pl.ds(0, rank)]
        norm = lax.rsqrt(jnp.mean(part * part, axis=1, keepdims=True) + epsilon)
        normed[...] = (part * norm * gain_ref[...]).astype(jnp.bfloat16)

    raw = product(normed[...], step_weight_ref[...]) + step_bias_ref[...]
    size = jnp.maximum(raw, 0.0) + jnp.log1p(jnp.exp(-jnp.abs(raw)))
    step[...] = size
    scaled[...] = size * activated_ref[...].astype(jnp.float32)
    rate[...] = jnp.exp(decay_ref[...]) * (-math.log2(math.e))
    lanes = 128

    tiles = width // lanes
    group = 8

    def body(index, _):
        first = pl.multiple_of((index // tiles) * group, group)
        at = pl.ds(pl.multiple_of((index % tiles) * lanes, lanes), lanes)
        fading = rate[:, at]
        sizes, inputs = [], []
        for t in range(tokens):
            rows = pl.ds(pl.multiple_of(t * slots + first, group), group)
            sizes.append(step[rows, at])
            inputs.append(scaled[rows, at])
        sums = [[] for _ in range(tokens)]
        for i in range(group):
            taken = accepted_ref[first + i]
            carried = state_ref[first + i, :, at].astype(jnp.float32)
            chosen = carried
            for t in range(tokens):
                row = t * slots + first + i
                fade = jnp.exp2(sizes[t][i : i + 1] * fading)
                carried = fade * carried + inputs[t][i : i + 1] * into_ref[row]
                sums[t].append(jnp.sum(outof_ref[row] * carried, axis=0, keepdims=True))
                chosen = jnp.where(taken == t + 1, carried, chosen)
            new_state_ref[first + i, :, at] = chosen.astype(jnp.bfloat16)
        for t in range(tokens):
            rows = pl.ds(pl.multiple_of(t * slots + first, group), group)
            result[rows, at] = jnp.concatenate(sums[t], axis=0)
        return 0

    lax.fori_loop(0, slots // group * tiles, body, 0)
    out_ref[...] = (
        result[...] + skip_ref[...] * activated_ref[...].astype(jnp.float32)
    ).astype(jnp.bfloat16)


def recur(
    slot_accepted,
    projected,
    step_gain,
    step_weight,
    step_bias,
    decay_log,
    skip_gain,
    activated,
    state_cache,
    tokens,
):
    slots, states, channels = state_cache.shape
    rows = activated.shape[0]
    rank = step_gain.shape[0]
    width = min(512, channels)
    lanes = 128
    into = jnp.broadcast_to(
        projected[:, rank : rank + states, None], (rows, states, lanes)
    )
    outof = jnp.broadcast_to(projected[:, rank + states :, None], (rows, states, lanes))
    whole = lambda shape: pl.BlockSpec(shape, lambda i, accepted: (0,) * len(shape))
    strip = lambda count: pl.BlockSpec((count, width), lambda i, accepted: (0, i))
    return pl.pallas_call(
        functools.partial(recur_kernel, tokens),
        out_shape=(
            jax.ShapeDtypeStruct((rows, channels), jnp.bfloat16),
            jax.ShapeDtypeStruct(state_cache.shape, jnp.bfloat16),
        ),
        grid_spec=pltpu.PrefetchScalarGridSpec(
            num_scalar_prefetch=1,
            grid=(channels // width,),
            in_specs=[
                whole(projected.shape),
                whole((1, rank)),
                strip(rank),
                strip(1),
                strip(states),
                strip(1),
                strip(rows),
                pl.BlockSpec((slots, states, width), lambda i, accepted: (0, 0, i)),
                whole((rows, states, lanes)),
                whole((rows, states, lanes)),
            ],
            out_specs=(
                strip(rows),
                pl.BlockSpec((slots, states, width), lambda i, accepted: (0, 0, i)),
            ),
            scratch_shapes=[
                pltpu.VMEM((rows, rank), jnp.bfloat16),
                pltpu.VMEM((rows, width), jnp.float32),
                pltpu.VMEM((rows, width), jnp.float32),
                pltpu.VMEM((rows, width), jnp.float32),
                pltpu.VMEM((states, width), jnp.float32),
            ],
        ),
        compiler_params=pltpu.CompilerParams(vmem_limit_bytes=VMEM_LIMIT),
    )(
        slot_accepted,
        projected,
        step_gain[None, :],
        step_weight,
        step_bias[None, :],
        decay_log,
        skip_gain[None, :],
        activated,
        state_cache,
        into,
        outof,
    )


def on_device(
    hidden_input,
    input_weight,
    kernel_weight,
    kernel_bias,
    select_weight,
    step_gain,
    step_weight,
    step_bias,
    decay_log,
    skip_gain,
    state_cache,
    window_cache,
    cache_owner,
    cache_slot,
    accepted,
):
    owner_count = lax.axis_size("dp")
    slots, states, channels = state_cache.shape
    kept = window_cache.shape[1]
    request_count = cache_owner.shape[0]
    tokens = hidden_input.shape[0] // request_count
    send_row, slot_source, slot_accepted, capacity = routing(
        cache_owner, cache_slot, accepted, slots
    )
    lines = lax.axis_size("tensor") // 2
    block = tokens * capacity
    token_axis = jnp.arange(tokens, dtype=jnp.int32)
    request_code = (send_row[:, None] * tokens + token_axis[None, :]).reshape(-1)
    base = (
        jnp.arange(capacity, dtype=jnp.int32)[None, :] * tokens + token_axis[:, None]
    ).reshape(-1)
    slot_code = jnp.where(
        slot_source[None, :] >= 0, slot_source[None, :] * tokens + token_axis[:, None], -1
    ).reshape(-1)
    inputs = project(
        hidden_input, input_weight, request_code, slot_code, base, owner_count, lines, block
    )
    activated, partial_value, rolled = mix(
        inputs,
        jnp.transpose(window_cache, (1, 0, 2)),
        kernel_weight,
        kernel_bias,
        select_weight.T,
        slot_accepted,
        tokens,
    )
    projected = lax.psum(partial_value, "tensor")
    outputs, new_state_cache = recur(
        slot_accepted,
        projected,
        step_gain,
        step_weight,
        step_bias,
        decay_log,
        skip_gain,
        activated,
        state_cache,
        tokens,
    )
    mamba_output = send_back(outputs, request_code, slot_code, base, owner_count, block)
    return mamba_output, new_state_cache, jnp.transpose(rolled, (1, 0, 2))


def solution(mesh):
    in_specs = (
        P(("groups", "dp"), "tensor"),
        P(None, "tensor"),
        P(None, "tensor"),
        P("tensor"),
        P("tensor", None),
        P(),
        P(None, "tensor"),
        P("tensor"),
        P(None, "tensor"),
        P("tensor"),
        P(("groups", "dp"), None, "tensor"),
        P(("groups", "dp"), None, "tensor"),
        P(("groups", "dp")),
        P(("groups", "dp")),
        P(("groups", "dp")),
    )
    out_specs = (
        P(("groups", "dp"), "tensor"),
        P(("groups", "dp"), None, "tensor"),
        P(("groups", "dp"), None, "tensor"),
    )
    return jax.shard_map(
        on_device, mesh=mesh, in_specs=in_specs, out_specs=out_specs, check_vma=False
    )
```

```python
import functools
import math

import jax
import jax.numpy as jnp
from jax import lax
from jax.experimental import pallas as pl
from jax.experimental.pallas import tpu as pltpu
from jax.sharding import PartitionSpec as P

epsilon = 1e-06


def routing(cache_owner, cache_slot, accepted, slots_here):
    owner_count = lax.axis_size("dp")
    here = lax.axis_index("dp")
    request_count = cache_owner.shape[0]
    capacity = 2 * request_count // owner_count
    place = cache_owner * slots_here + cache_slot
    everyone = lax.all_gather(place * 8 + accepted, "dp", axis=0, tiled=False)
    earlier = jnp.tril(jnp.ones((request_count, request_count), jnp.int32), -1)
    place_all = everyone // 8
    owner_all = place_all // slots_here
    same = (owner_all[:, :, None] == owner_all[:, None, :]).astype(jnp.int32)
    within_all = jnp.sum(same * earlier[None], axis=2)
    mine = (owner_all == here).reshape(-1)
    slot_all = jnp.where(mine, (place_all - here * slots_here).reshape(-1), -1)
    packed_all = (jnp.arange(owner_count)[:, None] * capacity + within_all).reshape(-1)
    match = slot_all[None, :] == jnp.arange(slots_here)[:, None]
    slot_source = jnp.max(jnp.where(match, packed_all[None, :], -1), axis=1)
    slot_accepted = jnp.max(jnp.where(match, (everyone % 8).reshape(-1)[None, :], 0), axis=1)
    own_same = (cache_owner[:, None] == cache_owner[None, :]).astype(jnp.int32)
    send_row = cache_owner * capacity + jnp.sum(own_same * earlier, axis=1)
    return send_row, slot_source, slot_accepted, capacity


MESH = pl.DeviceIdType.MESH
VMEM_LIMIT = 60 * 1024 * 1024


def match(left, right):
    return (left == right).astype(jnp.bfloat16)


def product(left, right):
    return jnp.dot(left, right, preferred_element_type=jnp.float32)


def project_kernel(
    sizes,
    hidden_ref,
    weight_ref,
    request_ref,
    slot_ref,
    base_col_ref,
    base_row_ref,
    out_ref,
    send,
    recv,
    gath,
    wbuf,
    acc,
    w_sem,
    z_send,
    z_recv,
    x_send,
    x_recv,
    s_send,
    s_recv,
):
    owners, lines, chunks, width, block, columns = sizes
    dp = lax.axis_index("dp")
    tensor = lax.axis_index("tensor")
    line = tensor // 2
    core = tensor % 2
    depth = width * chunks

    def origin(step):
        return ((line + lines - step // 2) % lines) * 2 + (core + step) % 2

    weights = []
    for k in range(chunks):
        for g in range(2 * lines):
            first = pl.multiple_of(origin(g) * depth + k * width, width)
            copy = pltpu.make_async_copy(
                weight_ref.at[pl.ds(first, width)], wbuf.at[k, g], w_sem.at[k, g]
            )
            copy.start()
            weights.append(copy)

    barrier = pltpu.get_barrier_semaphore()
    sibling = line * 2 + 1 - core
    pl.semaphore_signal(barrier, inc=1, device_id={"tensor": sibling}, device_id_type=MESH)
    for j in range(1, owners):
        pl.semaphore_signal(
            barrier, inc=1, device_id={"dp": (dp + j) % owners}, device_id_type=MESH
        )
    for j in range(1, lines):
        pl.semaphore_signal(
            barrier,
            inc=1,
            device_id={"tensor": ((line + j) % lines) * 2 + core},
            device_id_type=MESH,
        )
    pl.semaphore_wait(barrier, owners + lines - 1)

    across = {}
    for k in range(chunks):
        part = pl.ds(k * width, width)
        for j in list(range(1, owners)) + [0]:
            target = (dp + j) % owners
            pick = match(base_col_ref[...] + target * block, request_ref[...])
            rows = product(pick, hidden_ref[:, part]).astype(jnp.bfloat16)
            if j == 0:
                recv[k, 0] = rows
            else:
                send[k, j] = rows
                copy = pltpu.make_async_remote_copy(
                    src_ref=send.at[k, j],
                    dst_ref=recv.at[k, j],
                    send_sem=z_send.at[k, j],
                    recv_sem=z_recv.at[k, j],
                    device_id={"dp": target},
                    device_id_type=MESH,
                )
                copy.start()
                across[k, j] = copy

    strip = min(512, columns)

    def multiply(k, g):
        weights[k * 2 * lines + g].wait()

        def body(c, _):
            at = pl.ds(pl.multiple_of(c * strip, strip), strip)
            value = product(gath[k, g], wbuf[k, g, :, at])
            if k == 0 and g == 0:
                acc[:, at] = value
            else:
                acc[:, at] += value
            return 0

        lax.fori_loop(0, columns // strip, body, 0)

    sideways, shared = {}, {}

    def share(k, g):
        copy = pltpu.make_async_remote_copy(
            src_ref=gath.at[k, g],
            dst_ref=gath.at[k, g + 1],
            send_sem=s_send.at[k, g],
            recv_sem=s_recv.at[k, g],
            device_id={"tensor": sibling},
            device_id_type=MESH,
        )
        copy.start()
        shared[k, g] = copy

    def first(k):
        total = None
        for j in range(owners):
            if j:
                across[k, j].wait_recv()
            source = (dp + owners - j) % owners
            pick = match(slot_ref[...], base_row_ref[...] + source * block)
            value = product(pick, recv[k, j])
            total = value if total is None else total + value
        gath[k, 0] = total.astype(jnp.bfloat16)
        for j in range(1, lines):
            copy = pltpu.make_async_remote_copy(
                src_ref=gath.at[k, 0],
                dst_ref=gath.at[k, 2 * j],
                send_sem=x_send.at[k, j],
                recv_sem=x_recv.at[k, j],
                device_id={"tensor": ((line + j) % lines) * 2 + core},
                device_id_type=MESH,
            )
            copy.start()
            sideways[k, j] = copy
        share(k, 0)
        multiply(k, 0)

    def second(k):
        for j in range(1, lines):
            sideways[k, j].wait_recv()
            share(k, 2 * j)
        shared[k, 0].wait_recv()
        multiply(k, 1)
        for j in range(1, lines):
            multiply(k, 2 * j)

    def third(k):
        for j in range(1, lines):
            shared[k, 2 * j].wait_recv()
            multiply(k, 2 * j + 1)

    for step in range(chunks + 2):
        if step < chunks:
            first(step)
        if 1 <= step <= chunks:
            second(step - 1)
        if step >= 2:
            third(step - 2)
    out_ref[...] = acc[...].astype(jnp.bfloat16)
    for copy in list(across.values()) + list(sideways.values()) + list(shared.values()):
        copy.wait_send()


def project(hidden, weight, request_code, slot_code, base, owners, lines, block):
    rows, depth = hidden.shape
    columns = weight.shape[1]
    placed = slot_code.shape[0]
    chunks = 4
    width = depth // chunks
    groups = 2 * lines
    sizes = (owners, lines, chunks, width, block, columns)
    vmem = pl.BlockSpec(memory_space=pltpu.VMEM)
    dma = pltpu.SemaphoreType.DMA
    return pl.pallas_call(
        functools.partial(project_kernel, sizes),
        out_shape=jax.ShapeDtypeStruct((placed, columns), jnp.bfloat16),
        in_specs=[vmem, pl.BlockSpec(memory_space=pl.ANY)] + [vmem] * 4,
        out_specs=vmem,
        scratch_shapes=[
            pltpu.VMEM((chunks, owners, block, width), jnp.bfloat16),
            pltpu.VMEM((chunks, owners, block, width), jnp.bfloat16),
            pltpu.VMEM((chunks, groups, placed, width), jnp.bfloat16),
            pltpu.VMEM((chunks, groups, width, columns), jnp.bfloat16),
            pltpu.VMEM((placed, columns), jnp.float32),
            dma((chunks, groups)),
            dma((chunks, owners)),
            dma((chunks, owners)),
            dma((chunks, lines)),
            dma((chunks, lines)),
            dma((chunks, groups)),
            dma((chunks, groups)),
        ],
        compiler_params=pltpu.CompilerParams(
            collective_id=0, has_side_effects=True, vmem_limit_bytes=VMEM_LIMIT
        ),
        cost_estimate=pl.CostEstimate(
            flops=2 * placed * depth * groups * columns,
            bytes_accessed=2 * depth * groups * columns,
            transcendentals=0,
        ),
    )(hidden, weight, request_code[None, :], slot_code[:, None], base[:, None], base[None, :])


def return_kernel(
    sizes,
    rows_ref,
    request_ref,
    slot_ref,
    base_col_ref,
    base_row_ref,
    out_ref,
    send,
    recv,
    z_send,
    z_recv,
):
    owners, chunks, width, block = sizes
    dp = lax.axis_index("dp")
    barrier = pltpu.get_barrier_semaphore()
    for j in range(1, owners):
        pl.semaphore_signal(
            barrier, inc=1, device_id={"dp": (dp + j) % owners}, device_id_type=MESH
        )
    pl.semaphore_wait(barrier, owners - 1)
    across = {}
    for k in range(chunks):
        part = pl.ds(k * width, width)
        for j in list(range(1, owners)) + [0]:
            target = (dp + j) % owners
            pick = match(base_col_ref[...] + target * block, slot_ref[...])
            rows = product(pick, rows_ref[:, part]).astype(jnp.bfloat16)
            if j == 0:
                recv[k, 0] = rows
            else:
                send[k, j] = rows
                copy = pltpu.make_async_remote_copy(
                    src_ref=send.at[k, j],
                    dst_ref=recv.at[k, j],
                    send_sem=z_send.at[k, j],
                    recv_sem=z_recv.at[k, j],
                    device_id={"dp": target},
                    device_id_type=MESH,
                )
                copy.start()
                across[k, j] = copy
    for k in range(chunks):
        total = None
        for j in range(owners):
            if j:
                across[k, j].wait_recv()
            source = (dp + owners - j) % owners
            pick = match(request_ref[...], base_row_ref[...] + source * block)
            value = product(pick, recv[k, j])
            total = value if total is None else total + value
        out_ref[:, pl.ds(k * width, width)] = total.astype(jnp.bfloat16)
    for copy in across.values():
        copy.wait_send()


def send_back(rows, request_code, slot_code, base, owners, block):
    columns = rows.shape[1]
    chunks = 4
    width = columns // chunks
    vmem = pl.BlockSpec(memory_space=pltpu.VMEM)
    dma = pltpu.SemaphoreType.DMA
    return pl.pallas_call(
        functools.partial(return_kernel, (owners, chunks, width, block)),
        out_shape=jax.ShapeDtypeStruct((request_code.shape[0], columns), jnp.bfloat16),
        in_specs=[vmem] * 5,
        out_specs=vmem,
        scratch_shapes=[
            pltpu.VMEM((chunks, owners, block, width), jnp.bfloat16),
            pltpu.VMEM((chunks, owners, block, width), jnp.bfloat16),
            dma((chunks, owners)),
            dma((chunks, owners)),
        ],
        compiler_params=pltpu.CompilerParams(
            collective_id=1, has_side_effects=True, vmem_limit_bytes=VMEM_LIMIT
        ),
    )(rows, request_code[:, None], slot_code[None, :], base[:, None], base[None, :])


def mix_kernel(
    tokens,
    inputs_ref,
    window_ref,
    taps_ref,
    bias_ref,
    select_ref,
    accepted_ref,
    activated_ref,
    partial_ref,
    rolled_ref,
):
    kept, slots, width = window_ref.shape

    def row(position):
        if position < kept:
            return window_ref[position]
        return inputs_ref[pl.ds((position - kept) * slots, slots), :]

    window = [row(position) for position in range(kept + tokens)]
    wide = [value.astype(jnp.float32) for value in window]
    for t in range(tokens):
        mixed = bias_ref[...] + taps_ref[pl.ds(0, 1), :] * wide[t]
        for tap in range(1, taps_ref.shape[0]):
            mixed = mixed + taps_ref[pl.ds(tap, 1), :] * wide[t + tap]
        activated_ref[pl.ds(t * slots, slots), :] = (mixed * jax.nn.sigmoid(mixed)).astype(
            jnp.bfloat16
        )
    accepted = jnp.broadcast_to(accepted_ref[...], (slots, width))
    for place in range(kept):
        chosen = wide[place]
        for position in range(1, tokens + 1):
            chosen = jnp.where(accepted == position, wide[position + place], chosen)
        rolled_ref[place] = chosen.astype(jnp.bfloat16)
    value = lax.dot_general(
        activated_ref[...],
        select_ref[...],
        (((1,), (1,)), ((), ())),
        preferred_element_type=jnp.float32,
    )

    @pl.when(pl.program_id(0) == 0)
    def _():
        partial_ref[...] = value

    @pl.when(pl.program_id(0) > 0)
    def _():
        partial_ref[...] += value


def mix(inputs, window, kernel_weight, kernel_bias, select_rows, slot_accepted, tokens):
    kept, slots, channels = window.shape
    width = min(512, channels)
    return pl.pallas_call(
        functools.partial(mix_kernel, tokens),
        grid=(channels // width,),
        out_shape=(
            jax.ShapeDtypeStruct(inputs.shape, jnp.bfloat16),
            jax.ShapeDtypeStruct((inputs.shape[0], select_rows.shape[0]), jnp.float32),
            jax.ShapeDtypeStruct(window.shape, jnp.bfloat16),
        ),
        in_specs=[
            pl.BlockSpec((inputs.shape[0], width), lambda i: (0, i)),
            pl.BlockSpec((kept, slots, width), lambda i: (0, 0, i)),
            pl.BlockSpec((kernel_weight.shape[0], width), lambda i: (0, i)),
            pl.BlockSpec((1, width), lambda i: (0, i)),
            pl.BlockSpec((select_rows.shape[0], width), lambda i: (0, i)),
            pl.BlockSpec((slots, 1), lambda i: (0, 0)),
        ],
        out_specs=(
            pl.BlockSpec((inputs.shape[0], width), lambda i: (0, i)),
            pl.BlockSpec((inputs.shape[0], select_rows.shape[0]), lambda i: (0, 0)),
            pl.BlockSpec((kept, slots, width), lambda i: (0, 0, i)),
        ),
        compiler_params=pltpu.CompilerParams(vmem_limit_bytes=VMEM_LIMIT),
    )(inputs, window, kernel_weight, kernel_bias[None, :], select_rows, slot_accepted[:, None])


def total_kernel(
    sizes, mine_ref, out_ref, pair, held, lines_in, p_send, p_recv, x_send, x_recv, s_send, s_recv
):
    lines, pieces, piece = sizes
    tensor = lax.axis_index("tensor")
    line = tensor // 2
    core = tensor % 2
    sibling = line * 2 + 1 - core
    half = pieces * piece
    barrier = pltpu.get_barrier_semaphore()
    pl.semaphore_signal(barrier, inc=1, device_id={"tensor": sibling}, device_id_type=MESH)
    for j in range(1, lines):
        pl.semaphore_signal(
            barrier,
            inc=1,
            device_id={"tensor": ((line + j) % lines) * 2 + core},
            device_id_type=MESH,
        )
    pl.semaphore_wait(barrier, lines)

    def send(source, target, sends, arrives, device):
        copy = pltpu.make_async_remote_copy(
            src_ref=source,
            dst_ref=target,
            send_sem=sends,
            recv_sem=arrives,
            device_id={"tensor": device},
            device_id_type=MESH,
        )
        copy.start()
        return copy

    def rows(owner, p):
        return pl.ds(pl.multiple_of(owner * half + p * piece, 8), piece)

    paired = [
        send(mine_ref.at[rows(1 - core, p)], pair.at[p], p_send.at[p], p_recv.at[p], sibling)
        for p in range(pieces)
    ]
    crossed = {}
    for p in range(pieces):
        paired[p].wait_recv()
        held[p] = mine_ref[rows(core, p), :] + pair[p]
        for j in range(1, lines):
            crossed[p, j] = send(
                held.at[p],
                lines_in.at[p, j],
                x_send.at[p, j],
                x_recv.at[p, j],
                ((line + j) % lines) * 2 + core,
            )
    final = []
    for p in range(pieces):
        value = held[p]
        for j in range(1, lines):
            crossed[p, j].wait_recv()
            value = value + lines_in[p, j]
        out_ref[rows(core, p), :] = value
        final.append(
            send(
                out_ref.at[rows(core, p)],
                out_ref.at[rows(core, p)],
                s_send.at[p],
                s_recv.at[p],
                sibling,
            )
        )
    for copy in final:
        copy.wait_recv()
    for copy in paired + list(crossed.values()) + final:
        copy.wait_send()


def total(partial_value, lines):
    rows, columns = partial_value.shape
    pieces = 4
    piece = rows // (2 * pieces)
    vmem = pl.BlockSpec(memory_space=pltpu.VMEM)
    dma = pltpu.SemaphoreType.DMA
    return pl.pallas_call(
        functools.partial(total_kernel, (lines, pieces, piece)),
        out_shape=jax.ShapeDtypeStruct((rows, columns), jnp.float32),
        in_specs=[vmem],
        out_specs=vmem,
        scratch_shapes=[
            pltpu.VMEM((pieces, piece, columns), jnp.float32),
            pltpu.VMEM((pieces, piece, columns), jnp.float32),
            pltpu.VMEM((pieces, lines, piece, columns), jnp.float32),
            dma((pieces,)),
            dma((pieces,)),
            dma((pieces, lines)),
            dma((pieces, lines)),
            dma((pieces,)),
            dma((pieces,)),
        ],
        compiler_params=pltpu.CompilerParams(
            collective_id=2, has_side_effects=True, vmem_limit_bytes=VMEM_LIMIT
        ),
    )(partial_value)


def recur_kernel(
    tokens,
    accepted_ref,
    projected_ref,
    gain_ref,
    step_weight_ref,
    step_bias_ref,
    decay_ref,
    skip_ref,
    activated_ref,
    state_ref,
    into_ref,
    outof_ref,
    out_ref,
    new_state_ref,
    normed,
    step,
    scaled,
    result,
    rate,
):
    slots, states, width = state_ref.shape

    @pl.when(pl.program_id(0) == 0)
    def _():
        rank = gain_ref.shape[1]
        part = projected_ref[:, pl.ds(0, rank)]
        norm = lax.rsqrt(jnp.mean(part * part, axis=1, keepdims=True) + epsilon)
        normed[...] = (part * norm * gain_ref[...]).astype(jnp.bfloat16)

    raw = product(normed[...], step_weight_ref[...]) + step_bias_ref[...]
    size = jnp.maximum(raw, 0.0) + jnp.log1p(jnp.exp(-jnp.abs(raw)))
    step[...] = size
    scaled[...] = size * activated_ref[...].astype(jnp.float32)
    rate[...] = jnp.exp(decay_ref[...]) * (-math.log2(math.e))
    lanes = 128

    tiles = width // lanes
    group = 8

    def body(index, _):
        first = pl.multiple_of((index // tiles) * group, group)
        at = pl.ds(pl.multiple_of((index % tiles) * lanes, lanes), lanes)
        fading = rate[:, at]
        sizes, inputs = [], []
        for t in range(tokens):
            rows = pl.ds(pl.multiple_of(t * slots + first, group), group)
            sizes.append(step[rows, at])
            inputs.append(scaled[rows, at])
        sums = [[] for _ in range(tokens)]
        for i in range(group):
            taken = accepted_ref[first + i]
            carried = state_ref[first + i, :, at].astype(jnp.float32)
            chosen = carried
            for t in range(tokens):
                row = t * slots + first + i
                fade = jnp.exp2(sizes[t][i : i + 1] * fading)
                carried = fade * carried + inputs[t][i : i + 1] * into_ref[row]
                sums[t].append(jnp.sum(outof_ref[row] * carried, axis=0, keepdims=True))
                chosen = jnp.where(taken == t + 1, carried, chosen)
            new_state_ref[first + i, :, at] = chosen.astype(jnp.bfloat16)
        for t in range(tokens):
            rows = pl.ds(pl.multiple_of(t * slots + first, group), group)
            result[rows, at] = jnp.concatenate(sums[t], axis=0)
        return 0

    lax.fori_loop(0, slots // group * tiles, body, 0)
    out_ref[...] = (
        result[...] + skip_ref[...] * activated_ref[...].astype(jnp.float32)
    ).astype(jnp.bfloat16)


def recur(
    slot_accepted,
    projected,
    step_gain,
    step_weight,
    step_bias,
    decay_log,
    skip_gain,
    activated,
    state_cache,
    tokens,
):
    slots, states, channels = state_cache.shape
    rows = activated.shape[0]
    rank = step_gain.shape[0]
    width = min(512, channels)
    lanes = 128
    into = jnp.broadcast_to(
        projected[:, rank : rank + states, None], (rows, states, lanes)
    )
    outof = jnp.broadcast_to(projected[:, rank + states :, None], (rows, states, lanes))
    whole = lambda shape: pl.BlockSpec(shape, lambda i, accepted: (0,) * len(shape))
    strip = lambda count: pl.BlockSpec((count, width), lambda i, accepted: (0, i))
    return pl.pallas_call(
        functools.partial(recur_kernel, tokens),
        out_shape=(
            jax.ShapeDtypeStruct((rows, channels), jnp.bfloat16),
            jax.ShapeDtypeStruct(state_cache.shape, jnp.bfloat16),
        ),
        grid_spec=pltpu.PrefetchScalarGridSpec(
            num_scalar_prefetch=1,
            grid=(channels // width,),
            in_specs=[
                whole(projected.shape),
                whole((1, rank)),
                strip(rank),
                strip(1),
                strip(states),
                strip(1),
                strip(rows),
                pl.BlockSpec((slots, states, width), lambda i, accepted: (0, 0, i)),
                whole((rows, states, lanes)),
                whole((rows, states, lanes)),
            ],
            out_specs=(
                strip(rows),
                pl.BlockSpec((slots, states, width), lambda i, accepted: (0, 0, i)),
            ),
            scratch_shapes=[
                pltpu.VMEM((rows, rank), jnp.bfloat16),
                pltpu.VMEM((rows, width), jnp.float32),
                pltpu.VMEM((rows, width), jnp.float32),
                pltpu.VMEM((rows, width), jnp.float32),
                pltpu.VMEM((states, width), jnp.float32),
            ],
        ),
        compiler_params=pltpu.CompilerParams(vmem_limit_bytes=VMEM_LIMIT),
    )(
        slot_accepted,
        projected,
        step_gain[None, :],
        step_weight,
        step_bias[None, :],
        decay_log,
        skip_gain[None, :],
        activated,
        state_cache,
        into,
        outof,
    )


def on_device(
    hidden_input,
    input_weight,
    kernel_weight,
    kernel_bias,
    select_weight,
    step_gain,
    step_weight,
    step_bias,
    decay_log,
    skip_gain,
    state_cache,
    window_cache,
    cache_owner,
    cache_slot,
    accepted,
):
    owner_count = lax.axis_size("dp")
    slots, states, channels = state_cache.shape
    kept = window_cache.shape[1]
    request_count = cache_owner.shape[0]
    tokens = hidden_input.shape[0] // request_count
    send_row, slot_source, slot_accepted, capacity = routing(
        cache_owner, cache_slot, accepted, slots
    )
    lines = lax.axis_size("tensor") // 2
    block = tokens * capacity
    token_axis = jnp.arange(tokens, dtype=jnp.int32)
    request_code = (send_row[:, None] * tokens + token_axis[None, :]).reshape(-1)
    base = (
        jnp.arange(capacity, dtype=jnp.int32)[None, :] * tokens + token_axis[:, None]
    ).reshape(-1)
    slot_code = jnp.where(
        slot_source[None, :] >= 0, slot_source[None, :] * tokens + token_axis[:, None], -1
    ).reshape(-1)
    inputs = project(
        hidden_input, input_weight, request_code, slot_code, base, owner_count, lines, block
    )
    activated, partial_value, rolled = mix(
        inputs,
        jnp.transpose(window_cache, (1, 0, 2)),
        kernel_weight,
        kernel_bias,
        select_weight.T,
        slot_accepted,
        tokens,
    )
    projected = total(partial_value, lines)
    outputs, new_state_cache = recur(
        slot_accepted,
        projected,
        step_gain,
        step_weight,
        step_bias,
        decay_log,
        skip_gain,
        activated,
        state_cache,
        tokens,
    )
    mamba_output = send_back(outputs, request_code, slot_code, base, owner_count, block)
    return mamba_output, new_state_cache, jnp.transpose(rolled, (1, 0, 2))


def solution(mesh):
    in_specs = (
        P(("groups", "dp"), "tensor"),
        P(None, "tensor"),
        P(None, "tensor"),
        P("tensor"),
        P("tensor", None),
        P(),
        P(None, "tensor"),
        P("tensor"),
        P(None, "tensor"),
        P("tensor"),
        P(("groups", "dp"), None, "tensor"),
        P(("groups", "dp"), None, "tensor"),
        P(("groups", "dp")),
        P(("groups", "dp")),
        P(("groups", "dp")),
    )
    out_specs = (
        P(("groups", "dp"), "tensor"),
        P(("groups", "dp"), None, "tensor"),
        P(("groups", "dp"), None, "tensor"),
    )
    return jax.shard_map(
        on_device, mesh=mesh, in_specs=in_specs, out_specs=out_specs, check_vma=False
    )
```

```python
import functools
import math

import jax
import jax.numpy as jnp
from jax import lax
from jax.experimental import pallas as pl
from jax.experimental.pallas import tpu as pltpu
from jax.sharding import PartitionSpec as P

epsilon = 1e-06


def routing(cache_owner, cache_slot, accepted, slots_here):
    owner_count = lax.axis_size("dp")
    here = lax.axis_index("dp")
    request_count = cache_owner.shape[0]
    capacity = 2 * request_count // owner_count
    place = cache_owner * slots_here + cache_slot
    everyone = lax.all_gather(place * 8 + accepted, "dp", axis=0, tiled=False)
    earlier = jnp.tril(jnp.ones((request_count, request_count), jnp.int32), -1)
    place_all = everyone // 8
    owner_all = place_all // slots_here
    same = (owner_all[:, :, None] == owner_all[:, None, :]).astype(jnp.int32)
    within_all = jnp.sum(same * earlier[None], axis=2)
    mine = (owner_all == here).reshape(-1)
    slot_all = jnp.where(mine, (place_all - here * slots_here).reshape(-1), -1)
    packed_all = (jnp.arange(owner_count)[:, None] * capacity + within_all).reshape(-1)
    match = slot_all[None, :] == jnp.arange(slots_here)[:, None]
    slot_source = jnp.max(jnp.where(match, packed_all[None, :], -1), axis=1)
    slot_accepted = jnp.max(jnp.where(match, (everyone % 8).reshape(-1)[None, :], 0), axis=1)
    own_same = (cache_owner[:, None] == cache_owner[None, :]).astype(jnp.int32)
    send_row = cache_owner * capacity + jnp.sum(own_same * earlier, axis=1)
    return send_row, slot_source, slot_accepted, capacity


MESH = pl.DeviceIdType.MESH
VMEM_LIMIT = 60 * 1024 * 1024


def match(left, right):
    return (left == right).astype(jnp.bfloat16)


def product(left, right):
    return jnp.dot(left, right, preferred_element_type=jnp.float32)


def project_kernel(
    sizes,
    hidden_ref,
    weight_ref,
    request_ref,
    slot_ref,
    base_col_ref,
    base_row_ref,
    out_ref,
    send,
    recv,
    gath,
    wbuf,
    acc,
    w_sem,
    z_send,
    z_recv,
    x_send,
    x_recv,
    s_send,
    s_recv,
):
    owners, lines, chunks, width, block, columns = sizes
    dp = lax.axis_index("dp")
    tensor = lax.axis_index("tensor")
    line = tensor // 2
    core = tensor % 2
    depth = width * chunks

    def origin(step):
        return ((line + lines - step // 2) % lines) * 2 + (core + step) % 2

    weights = []
    for k in range(chunks):
        for g in range(2 * lines):
            first = pl.multiple_of(origin(g) * depth + k * width, width)
            copy = pltpu.make_async_copy(
                weight_ref.at[pl.ds(first, width)], wbuf.at[k, g], w_sem.at[k, g]
            )
            copy.start()
            weights.append(copy)

    barrier = pltpu.get_barrier_semaphore()
    sibling = line * 2 + 1 - core
    pl.semaphore_signal(barrier, inc=1, device_id={"tensor": sibling}, device_id_type=MESH)
    for j in range(1, owners):
        pl.semaphore_signal(
            barrier, inc=1, device_id={"dp": (dp + j) % owners}, device_id_type=MESH
        )
    for j in range(1, lines):
        pl.semaphore_signal(
            barrier,
            inc=1,
            device_id={"tensor": ((line + j) % lines) * 2 + core},
            device_id_type=MESH,
        )
    pl.semaphore_wait(barrier, owners + lines - 1)

    across = {}
    for k in range(chunks):
        part = pl.ds(k * width, width)
        for j in list(range(1, owners)) + [0]:
            target = (dp + j) % owners
            pick = match(base_col_ref[...] + target * block, request_ref[...])
            rows = product(pick, hidden_ref[:, part]).astype(jnp.bfloat16)
            if j == 0:
                recv[k, 0] = rows
            else:
                send[k, j] = rows
                copy = pltpu.make_async_remote_copy(
                    src_ref=send.at[k, j],
                    dst_ref=recv.at[k, j],
                    send_sem=z_send.at[k, j],
                    recv_sem=z_recv.at[k, j],
                    device_id={"dp": target},
                    device_id_type=MESH,
                )
                copy.start()
                across[k, j] = copy

    strip = min(512, columns)

    def multiply(k, g):
        weights[k * 2 * lines + g].wait()

        def body(c, _):
            at = pl.ds(pl.multiple_of(c * strip, strip), strip)
            value = product(gath[k, g], wbuf[k, g, :, at])
            if k == 0 and g == 0:
                acc[:, at] = value
            else:
                acc[:, at] += value
            return 0

        lax.fori_loop(0, columns // strip, body, 0)

    sideways, shared = {}, {}

    def share(k, g):
        copy = pltpu.make_async_remote_copy(
            src_ref=gath.at[k, g],
            dst_ref=gath.at[k, g + 1],
            send_sem=s_send.at[k, g],
            recv_sem=s_recv.at[k, g],
            device_id={"tensor": sibling},
            device_id_type=MESH,
        )
        copy.start()
        shared[k, g] = copy

    def first(k):
        total = None
        for j in range(owners):
            if j:
                across[k, j].wait_recv()
            source = (dp + owners - j) % owners
            pick = match(slot_ref[...], base_row_ref[...] + source * block)
            value = product(pick, recv[k, j])
            total = value if total is None else total + value
        gath[k, 0] = total.astype(jnp.bfloat16)
        for j in range(1, lines):
            copy = pltpu.make_async_remote_copy(
                src_ref=gath.at[k, 0],
                dst_ref=gath.at[k, 2 * j],
                send_sem=x_send.at[k, j],
                recv_sem=x_recv.at[k, j],
                device_id={"tensor": ((line + j) % lines) * 2 + core},
                device_id_type=MESH,
            )
            copy.start()
            sideways[k, j] = copy
        share(k, 0)
        multiply(k, 0)

    def second(k):
        for j in range(1, lines):
            sideways[k, j].wait_recv()
            share(k, 2 * j)
        shared[k, 0].wait_recv()
        multiply(k, 1)
        for j in range(1, lines):
            multiply(k, 2 * j)

    def third(k):
        for j in range(1, lines):
            shared[k, 2 * j].wait_recv()
            multiply(k, 2 * j + 1)

    for step in range(chunks + 2):
        if step < chunks:
            first(step)
        if 1 <= step <= chunks:
            second(step - 1)
        if step >= 2:
            third(step - 2)
    out_ref[...] = acc[...].astype(jnp.bfloat16)
    for copy in list(across.values()) + list(sideways.values()) + list(shared.values()):
        copy.wait_send()


def project(hidden, weight, request_code, slot_code, base, owners, lines, block):
    rows, depth = hidden.shape
    columns = weight.shape[1]
    placed = slot_code.shape[0]
    chunks = max(1, depth // 256)
    width = depth // chunks
    groups = 2 * lines
    sizes = (owners, lines, chunks, width, block, columns)
    vmem = pl.BlockSpec(memory_space=pltpu.VMEM)
    dma = pltpu.SemaphoreType.DMA
    return pl.pallas_call(
        functools.partial(project_kernel, sizes),
        out_shape=jax.ShapeDtypeStruct((placed, columns), jnp.bfloat16),
        in_specs=[vmem, pl.BlockSpec(memory_space=pl.ANY)] + [vmem] * 4,
        out_specs=vmem,
        scratch_shapes=[
            pltpu.VMEM((chunks, owners, block, width), jnp.bfloat16),
            pltpu.VMEM((chunks, owners, block, width), jnp.bfloat16),
            pltpu.VMEM((chunks, groups, placed, width), jnp.bfloat16),
            pltpu.VMEM((chunks, groups, width, columns), jnp.bfloat16),
            pltpu.VMEM((placed, columns), jnp.float32),
            dma((chunks, groups)),
            dma((chunks, owners)),
            dma((chunks, owners)),
            dma((chunks, lines)),
            dma((chunks, lines)),
            dma((chunks, groups)),
            dma((chunks, groups)),
        ],
        compiler_params=pltpu.CompilerParams(
            collective_id=0, has_side_effects=True, vmem_limit_bytes=VMEM_LIMIT
        ),
        cost_estimate=pl.CostEstimate(
            flops=2 * placed * depth * groups * columns,
            bytes_accessed=2 * depth * groups * columns,
            transcendentals=0,
        ),
    )(hidden, weight, request_code[None, :], slot_code[:, None], base[:, None], base[None, :])


def return_kernel(
    sizes,
    rows_ref,
    request_ref,
    slot_ref,
    base_col_ref,
    base_row_ref,
    out_ref,
    send,
    recv,
    z_send,
    z_recv,
):
    owners, chunks, width, block = sizes
    dp = lax.axis_index("dp")
    barrier = pltpu.get_barrier_semaphore()
    for j in range(1, owners):
        pl.semaphore_signal(
            barrier, inc=1, device_id={"dp": (dp + j) % owners}, device_id_type=MESH
        )
    pl.semaphore_wait(barrier, owners - 1)
    across = {}
    for k in range(chunks):
        part = pl.ds(k * width, width)
        for j in list(range(1, owners)) + [0]:
            target = (dp + j) % owners
            pick = match(base_col_ref[...] + target * block, slot_ref[...])
            rows = product(pick, rows_ref[:, part]).astype(jnp.bfloat16)
            if j == 0:
                recv[k, 0] = rows
            else:
                send[k, j] = rows
                copy = pltpu.make_async_remote_copy(
                    src_ref=send.at[k, j],
                    dst_ref=recv.at[k, j],
                    send_sem=z_send.at[k, j],
                    recv_sem=z_recv.at[k, j],
                    device_id={"dp": target},
                    device_id_type=MESH,
                )
                copy.start()
                across[k, j] = copy
    for k in range(chunks):
        total = None
        for j in range(owners):
            if j:
                across[k, j].wait_recv()
            source = (dp + owners - j) % owners
            pick = match(request_ref[...], base_row_ref[...] + source * block)
            value = product(pick, recv[k, j])
            total = value if total is None else total + value
        out_ref[:, pl.ds(k * width, width)] = total.astype(jnp.bfloat16)
    for copy in across.values():
        copy.wait_send()


def send_back(rows, request_code, slot_code, base, owners, block):
    columns = rows.shape[1]
    chunks = max(1, columns // 256)
    width = columns // chunks
    vmem = pl.BlockSpec(memory_space=pltpu.VMEM)
    dma = pltpu.SemaphoreType.DMA
    return pl.pallas_call(
        functools.partial(return_kernel, (owners, chunks, width, block)),
        out_shape=jax.ShapeDtypeStruct((request_code.shape[0], columns), jnp.bfloat16),
        in_specs=[vmem] * 5,
        out_specs=vmem,
        scratch_shapes=[
            pltpu.VMEM((chunks, owners, block, width), jnp.bfloat16),
            pltpu.VMEM((chunks, owners, block, width), jnp.bfloat16),
            dma((chunks, owners)),
            dma((chunks, owners)),
        ],
        compiler_params=pltpu.CompilerParams(
            collective_id=1, has_side_effects=True, vmem_limit_bytes=VMEM_LIMIT
        ),
    )(rows, request_code[:, None], slot_code[None, :], base[:, None], base[None, :])


def mix_kernel(
    tokens,
    inputs_ref,
    window_ref,
    taps_ref,
    bias_ref,
    select_ref,
    accepted_ref,
    activated_ref,
    partial_ref,
    rolled_ref,
):
    kept, slots, width = window_ref.shape

    def row(position):
        if position < kept:
            return window_ref[position]
        return inputs_ref[pl.ds((position - kept) * slots, slots), :]

    window = [row(position) for position in range(kept + tokens)]
    wide = [value.astype(jnp.float32) for value in window]
    for t in range(tokens):
        mixed = bias_ref[...] + taps_ref[pl.ds(0, 1), :] * wide[t]
        for tap in range(1, taps_ref.shape[0]):
            mixed = mixed + taps_ref[pl.ds(tap, 1), :] * wide[t + tap]
        activated_ref[pl.ds(t * slots, slots), :] = (mixed * jax.nn.sigmoid(mixed)).astype(
            jnp.bfloat16
        )
    accepted = jnp.broadcast_to(accepted_ref[...], (slots, width))
    for place in range(kept):
        chosen = wide[place]
        for position in range(1, tokens + 1):
            chosen = jnp.where(accepted == position, wide[position + place], chosen)
        rolled_ref[place] = chosen.astype(jnp.bfloat16)
    value = lax.dot_general(
        activated_ref[...],
        select_ref[...],
        (((1,), (1,)), ((), ())),
        preferred_element_type=jnp.float32,
    )

    @pl.when(pl.program_id(0) == 0)
    def _():
        partial_ref[...] = value

    @pl.when(pl.program_id(0) > 0)
    def _():
        partial_ref[...] += value


def mix(inputs, window, kernel_weight, kernel_bias, select_rows, slot_accepted, tokens):
    kept, slots, channels = window.shape
    width = min(512, channels)
    return pl.pallas_call(
        functools.partial(mix_kernel, tokens),
        grid=(channels // width,),
        out_shape=(
            jax.ShapeDtypeStruct(inputs.shape, jnp.bfloat16),
            jax.ShapeDtypeStruct((inputs.shape[0], select_rows.shape[0]), jnp.float32),
            jax.ShapeDtypeStruct(window.shape, jnp.bfloat16),
        ),
        in_specs=[
            pl.BlockSpec((inputs.shape[0], width), lambda i: (0, i)),
            pl.BlockSpec((kept, slots, width), lambda i: (0, 0, i)),
            pl.BlockSpec((kernel_weight.shape[0], width), lambda i: (0, i)),
            pl.BlockSpec((1, width), lambda i: (0, i)),
            pl.BlockSpec((select_rows.shape[0], width), lambda i: (0, i)),
            pl.BlockSpec((slots, 1), lambda i: (0, 0)),
        ],
        out_specs=(
            pl.BlockSpec((inputs.shape[0], width), lambda i: (0, i)),
            pl.BlockSpec((inputs.shape[0], select_rows.shape[0]), lambda i: (0, 0)),
            pl.BlockSpec((kept, slots, width), lambda i: (0, 0, i)),
        ),
        compiler_params=pltpu.CompilerParams(vmem_limit_bytes=VMEM_LIMIT),
    )(inputs, window, kernel_weight, kernel_bias[None, :], select_rows, slot_accepted[:, None])


def total_kernel(
    sizes, mine_ref, out_ref, pair, held, lines_in, p_send, p_recv, x_send, x_recv, s_send, s_recv
):
    lines, pieces, piece = sizes
    tensor = lax.axis_index("tensor")
    line = tensor // 2
    core = tensor % 2
    sibling = line * 2 + 1 - core
    half = pieces * piece
    barrier = pltpu.get_barrier_semaphore()
    pl.semaphore_signal(barrier, inc=1, device_id={"tensor": sibling}, device_id_type=MESH)
    for j in range(1, lines):
        pl.semaphore_signal(
            barrier,
            inc=1,
            device_id={"tensor": ((line + j) % lines) * 2 + core},
            device_id_type=MESH,
        )
    pl.semaphore_wait(barrier, lines)

    def send(source, target, sends, arrives, device):
        copy = pltpu.make_async_remote_copy(
            src_ref=source,
            dst_ref=target,
            send_sem=sends,
            recv_sem=arrives,
            device_id={"tensor": device},
            device_id_type=MESH,
        )
        copy.start()
        return copy

    def rows(owner, p):
        return pl.ds(pl.multiple_of(owner * half + p * piece, 8), piece)

    paired = [
        send(mine_ref.at[rows(1 - core, p)], pair.at[p], p_send.at[p], p_recv.at[p], sibling)
        for p in range(pieces)
    ]
    crossed = {}
    for p in range(pieces):
        paired[p].wait_recv()
        held[p] = mine_ref[rows(core, p), :] + pair[p]
        for j in range(1, lines):
            crossed[p, j] = send(
                held.at[p],
                lines_in.at[p, j],
                x_send.at[p, j],
                x_recv.at[p, j],
                ((line + j) % lines) * 2 + core,
            )
    final = []
    for p in range(pieces):
        value = held[p]
        for j in range(1, lines):
            crossed[p, j].wait_recv()
            value = value + lines_in[p, j]
        out_ref[rows(core, p), :] = value
        final.append(
            send(
                out_ref.at[rows(core, p)],
                out_ref.at[rows(core, p)],
                s_send.at[p],
                s_recv.at[p],
                sibling,
            )
        )
    for copy in final:
        copy.wait_recv()
    for copy in paired + list(crossed.values()) + final:
        copy.wait_send()


def total(partial_value, lines):
    rows, columns = partial_value.shape
    pieces = 4
    piece = rows // (2 * pieces)
    vmem = pl.BlockSpec(memory_space=pltpu.VMEM)
    dma = pltpu.SemaphoreType.DMA
    return pl.pallas_call(
        functools.partial(total_kernel, (lines, pieces, piece)),
        out_shape=jax.ShapeDtypeStruct((rows, columns), jnp.float32),
        in_specs=[vmem],
        out_specs=vmem,
        scratch_shapes=[
            pltpu.VMEM((pieces, piece, columns), jnp.float32),
            pltpu.VMEM((pieces, piece, columns), jnp.float32),
            pltpu.VMEM((pieces, lines, piece, columns), jnp.float32),
            dma((pieces,)),
            dma((pieces,)),
            dma((pieces, lines)),
            dma((pieces, lines)),
            dma((pieces,)),
            dma((pieces,)),
        ],
        compiler_params=pltpu.CompilerParams(
            collective_id=2, has_side_effects=True, vmem_limit_bytes=VMEM_LIMIT
        ),
    )(partial_value)


def recur_kernel(
    tokens,
    accepted_ref,
    projected_ref,
    gain_ref,
    step_weight_ref,
    step_bias_ref,
    decay_ref,
    skip_ref,
    activated_ref,
    state_ref,
    into_ref,
    outof_ref,
    out_ref,
    new_state_ref,
    normed,
    step,
    scaled,
    result,
    rate,
):
    slots, states, width = state_ref.shape

    @pl.when(pl.program_id(0) == 0)
    def _():
        rank = gain_ref.shape[1]
        part = projected_ref[:, pl.ds(0, rank)]
        norm = lax.rsqrt(jnp.mean(part * part, axis=1, keepdims=True) + epsilon)
        normed[...] = (part * norm * gain_ref[...]).astype(jnp.bfloat16)

    raw = product(normed[...], step_weight_ref[...]) + step_bias_ref[...]
    size = jnp.maximum(raw, 0.0) + jnp.log1p(jnp.exp(-jnp.abs(raw)))
    step[...] = size
    scaled[...] = size * activated_ref[...].astype(jnp.float32)
    rate[...] = jnp.exp(decay_ref[...]) * (-math.log2(math.e))
    lanes = 128

    tiles = width // lanes
    group = 8

    def body(index, _):
        first = pl.multiple_of((index // tiles) * group, group)
        at = pl.ds(pl.multiple_of((index % tiles) * lanes, lanes), lanes)
        fading = rate[:, at]
        sizes, inputs = [], []
        for t in range(tokens):
            rows = pl.ds(pl.multiple_of(t * slots + first, group), group)
            sizes.append(step[rows, at])
            inputs.append(scaled[rows, at])
        sums = [[] for _ in range(tokens)]
        for i in range(group):
            taken = accepted_ref[first + i]
            carried = state_ref[first + i, :, at].astype(jnp.float32)
            chosen = carried
            for t in range(tokens):
                row = t * slots + first + i
                fade = jnp.exp2(sizes[t][i : i + 1] * fading)
                carried = fade * carried + inputs[t][i : i + 1] * into_ref[row]
                sums[t].append(jnp.sum(outof_ref[row] * carried, axis=0, keepdims=True))
                chosen = jnp.where(taken == t + 1, carried, chosen)
            new_state_ref[first + i, :, at] = chosen.astype(jnp.bfloat16)
        for t in range(tokens):
            rows = pl.ds(pl.multiple_of(t * slots + first, group), group)
            result[rows, at] = jnp.concatenate(sums[t], axis=0)
        return 0

    lax.fori_loop(0, slots // group * tiles, body, 0)
    out_ref[...] = (
        result[...] + skip_ref[...] * activated_ref[...].astype(jnp.float32)
    ).astype(jnp.bfloat16)


def recur(
    slot_accepted,
    projected,
    step_gain,
    step_weight,
    step_bias,
    decay_log,
    skip_gain,
    activated,
    state_cache,
    tokens,
):
    slots, states, channels = state_cache.shape
    rows = activated.shape[0]
    rank = step_gain.shape[0]
    width = min(512, channels)
    lanes = 128
    into = jnp.broadcast_to(
        projected[:, rank : rank + states, None], (rows, states, lanes)
    )
    outof = jnp.broadcast_to(projected[:, rank + states :, None], (rows, states, lanes))
    whole = lambda shape: pl.BlockSpec(shape, lambda i, accepted: (0,) * len(shape))
    strip = lambda count: pl.BlockSpec((count, width), lambda i, accepted: (0, i))
    return pl.pallas_call(
        functools.partial(recur_kernel, tokens),
        out_shape=(
            jax.ShapeDtypeStruct((rows, channels), jnp.bfloat16),
            jax.ShapeDtypeStruct(state_cache.shape, jnp.bfloat16),
        ),
        grid_spec=pltpu.PrefetchScalarGridSpec(
            num_scalar_prefetch=1,
            grid=(channels // width,),
            in_specs=[
                whole(projected.shape),
                whole((1, rank)),
                strip(rank),
                strip(1),
                strip(states),
                strip(1),
                strip(rows),
                pl.BlockSpec((slots, states, width), lambda i, accepted: (0, 0, i)),
                whole((rows, states, lanes)),
                whole((rows, states, lanes)),
            ],
            out_specs=(
                strip(rows),
                pl.BlockSpec((slots, states, width), lambda i, accepted: (0, 0, i)),
            ),
            scratch_shapes=[
                pltpu.VMEM((rows, rank), jnp.bfloat16),
                pltpu.VMEM((rows, width), jnp.float32),
                pltpu.VMEM((rows, width), jnp.float32),
                pltpu.VMEM((rows, width), jnp.float32),
                pltpu.VMEM((states, width), jnp.float32),
            ],
        ),
        compiler_params=pltpu.CompilerParams(vmem_limit_bytes=VMEM_LIMIT),
    )(
        slot_accepted,
        projected,
        step_gain[None, :],
        step_weight,
        step_bias[None, :],
        decay_log,
        skip_gain[None, :],
        activated,
        state_cache,
        into,
        outof,
    )


def on_device(
    hidden_input,
    input_weight,
    kernel_weight,
    kernel_bias,
    select_weight,
    step_gain,
    step_weight,
    step_bias,
    decay_log,
    skip_gain,
    state_cache,
    window_cache,
    cache_owner,
    cache_slot,
    accepted,
):
    owner_count = lax.axis_size("dp")
    slots, states, channels = state_cache.shape
    kept = window_cache.shape[1]
    request_count = cache_owner.shape[0]
    tokens = hidden_input.shape[0] // request_count
    send_row, slot_source, slot_accepted, capacity = routing(
        cache_owner, cache_slot, accepted, slots
    )
    lines = lax.axis_size("tensor") // 2
    block = tokens * capacity
    token_axis = jnp.arange(tokens, dtype=jnp.int32)
    request_code = (send_row[:, None] * tokens + token_axis[None, :]).reshape(-1)
    base = (
        jnp.arange(capacity, dtype=jnp.int32)[None, :] * tokens + token_axis[:, None]
    ).reshape(-1)
    slot_code = jnp.where(
        slot_source[None, :] >= 0, slot_source[None, :] * tokens + token_axis[:, None], -1
    ).reshape(-1)
    inputs = project(
        hidden_input, input_weight, request_code, slot_code, base, owner_count, lines, block
    )
    activated, partial_value, rolled = mix(
        inputs,
        jnp.transpose(window_cache, (1, 0, 2)),
        kernel_weight,
        kernel_bias,
        select_weight.T,
        slot_accepted,
        tokens,
    )
    projected = total(partial_value, lines)
    outputs, new_state_cache = recur(
        slot_accepted,
        projected,
        step_gain,
        step_weight,
        step_bias,
        decay_log,
        skip_gain,
        activated,
        state_cache,
        tokens,
    )
    mamba_output = send_back(outputs, request_code, slot_code, base, owner_count, block)
    return mamba_output, new_state_cache, jnp.transpose(rolled, (1, 0, 2))


def solution(mesh):
    in_specs = (
        P(("groups", "dp"), "tensor"),
        P(None, "tensor"),
        P(None, "tensor"),
        P("tensor"),
        P("tensor", None),
        P(),
        P(None, "tensor"),
        P("tensor"),
        P(None, "tensor"),
        P("tensor"),
        P(("groups", "dp"), None, "tensor"),
        P(("groups", "dp"), None, "tensor"),
        P(("groups", "dp")),
        P(("groups", "dp")),
        P(("groups", "dp")),
    )
    out_specs = (
        P(("groups", "dp"), "tensor"),
        P(("groups", "dp"), None, "tensor"),
        P(("groups", "dp"), None, "tensor"),
    )
    return jax.shard_map(
        on_device, mesh=mesh, in_specs=in_specs, out_specs=out_specs, check_vma=False
    )
```
